32 devices in a mesh: groups: 2 (over y), view: 16 (over z, x, core).
Axes of the slice: x: 2, y: 2, z: 4, core: 2. Of those that a mesh axis runs over, the one named last changes fastest.
Arguments:
- embeddings: bfloat16 [32, 1024, 768], P(('groups', 'view')), parts along dimension 0, may hold values from -6 to 6
- projection: bfloat16 [768, 768], replicated, may hold values from -0.21875 to 0.21875
- owners: int32 [32, 128, 1], P(('groups', 'view')), parts along dimension 0, may hold values from 0 to 15; in each aligned block of 128 rows (0 to 127, 128 to 255, ..., all dimensions but the last counted through in order) at most 16 rows name the same one
- local_blocks: int32 [32, 128], P(('groups', 'view')), parts along dimension 0, may hold values from 0 to 63
- patches: int32 [32, 4, 2048], P(('groups', 'view')), parts along dimension 0, may hold values from 0 to 1023
- weights: float32 [32, 4, 2048], P(('groups', 'view')), parts along dimension 0, may hold values from 0.05 to 1
Outputs:
- targets: bfloat16 [32768, 768], P(('groups', 'view')), parts along dimension 0
The draws below stay inside these ranges and needn't reach their ends.
There are 2 independent parts, one for each index of `groups`. The reference program is written for one: setup_inputs(seed, part) draws one part's arguments, and reference() takes and returns one part's arrays. A program takes and returns all parts, laid end to end along the dimension named above; an argument that names none is the same for every part. Nothing has to cross between parts.
Inputs may be any that keep to these rules, and one draw needn't show every extreme that they name: `owners`: among the 128 slots of one view, at most 16 name one owner; this is reached.
All inputs are finite; a program needn't handle non-finite values.
Results may differ from the reference program's by a relative error of at most 0.014.
Values may be sent and summed in bfloat16 or wider, within the bound.
A program may use at most 64 MiB of HBM per device.

```python
import math
import jax
import jax.numpy as jnp
import numpy as np
from jax import lax

D = 768
P_SIZE = 1024
BS = 16
VIS = 128
BLK_DEV = 64
VIEWS = 16
BLOCKS = 1024
CAP = 16
N_VIEW = 16


def touch_ends(drawn, own_key, smallest, top_value):
    extent = drawn.shape
    spot = [jax.random.randint(jax.random.fold_in(own_key, axis), (), 0, extent[axis]) for axis in range(len(extent))]
    drawn = drawn.at[tuple(spot)].set(smallest)
    longest = extent.index(max(extent))
    spot[longest] = (spot[longest] + 1) % extent[longest]
    return drawn.at[tuple(spot)].set(top_value)


def shard_levels(rng, dims, shards, least, largest):
    factor_of = 1.0
    for dim, shards_of in shards:
        steps = jax.random.uniform(jax.random.fold_in(jax.random.fold_in(rng, 6), dim), (shards_of,), jnp.float32, least / len(shards), largest / len(shards))
        factor_of = factor_of * jnp.repeat(jnp.exp(steps), dims[dim] // shards_of).reshape((-1,) + (1,) * (len(dims) - 1 - dim))
    return factor_of


def deal_out(own_key, own, number, rows, number_of, top, most, lean):
    order = jax.random.permutation(own_key, number_of)
    packed, common = shares(number_of, rows * top, most, lean, True), shares(number_of, rows * top, most, lean, False)
    places = jnp.arange(number_of)

    def named(lengths, rotation):
        used = int((lengths > 0).sum())
        fixed = max(1, used // 4)
        shifted = fixed + (places - fixed + rotation * (used - fixed)) % max(1, number_of - fixed)
        return jnp.zeros((number_of,), jnp.int32).at[order[jnp.where(places < fixed, places, shifted)]].set(jnp.asarray(lengths, jnp.int32))

    lengths = jnp.where(number % 4 == 0, named(packed, number // 4), named(common, number - number // 4 - 1))
    mixed = jax.random.permutation(jax.random.fold_in(own, 3), number_of)
    source_of, sink = mixed[0:number_of // 2 * 2:2], mixed[1:number_of // 2 * 2:2]
    room = jnp.minimum(lengths[source_of] - 1, most - lengths[sink]) // 2
    room = jnp.where((source_of == order[0]) | (sink == order[0]) | (lengths[sink] == 0), 0, jnp.maximum(room, 0))
    shifted = jax.random.randint(jax.random.fold_in(own, 4), (number_of // 2,), 0, 1 << 20) % (room + 1)
    lengths = lengths.at[source_of].add(-shifted).at[sink].add(shifted)
    labels = jnp.searchsorted(jnp.cumsum(lengths), jnp.arange(rows * top), side="right").astype(jnp.int32)
    listing = labels.reshape(top, rows).T
    listing = listing[jax.random.permutation(jax.random.fold_in(own, 1), rows)]
    rotation = jax.random.randint(jax.random.fold_in(own, 2), (rows, 1), 0, top)
    return jnp.take_along_axis(listing, (jnp.arange(top)[None, :] + rotation) % top, axis=1)


def shares(count, total, reach, skew, full):
    portions = [(1 << 20) // math.isqrt(rank ** skew) + 1 for rank in range(1, count + 1)]
    largest = reach if full else min(reach, max(-(-total // count), total * portions[0] // sum(portions)))
    least = 1 if total - largest >= count - 1 else 0
    counts, spare = [largest] + [least] * (count - 1), total - largest - least * (count - 1)
    while spare > 0:
        free = [i for i in range(1, count) if counts[i] < largest] or [i for i in range(1, count) if counts[i] < reach]
        mass, left = sum([portions[i] for i in free]), spare
        for i in free:
            addition = min(reach - counts[i], max(1, left * portions[i] // mass), spare)
            counts[i] = counts[i] + addition
            spare = spare - addition
    return np.array(counts)


def normal_values(own_key, shape, spread, bound, shards=(), kind=jnp.bfloat16):
    factor_of = shard_levels(own_key, shape, shards, -0.22, 0.18) if shards else 1.0
    values = jax.random.normal(own_key, shape, jnp.float32) * spread * factor_of
    return jnp.minimum(jnp.maximum(values, -bound), bound).astype(kind)


def setup_inputs(seed: int = 0, part: int = 0) -> dict:
    seeds = jax.random.split(jax.random.key(seed), 7)
    part_splits = jax.random.split(jax.random.fold_in(seeds[6], part), 7)
    embeddings = normal_values(part_splits[0], (VIEWS, P_SIZE, D), 1.0, 6.0, ((0, 16),))
    projection = normal_values(seeds[1], (D, D), D ** -0.5, 0.21875)
    owners_keys = jax.random.split(jax.random.fold_in(part_splits[2], 1), VIEWS * VIS // VIS)
    owners_turns = jax.random.permutation(jax.random.fold_in(part_splits[2], 3), VIEWS * VIS // VIS)
    owners = jax.vmap(lambda own, number: deal_out(jax.random.fold_in(part_splits[2], 2), own, number, VIS, N_VIEW, 1, CAP, 2))(owners_keys, owners_turns).reshape((VIEWS, VIS, 1))
    local_blocks = touch_ends(jax.random.randint(part_splits[3], (VIEWS, VIS), 0, BLK_DEV), jax.random.fold_in(part_splits[3], 1), 0, BLK_DEV - 1).astype(jnp.int32)
    patches = touch_ends(jax.random.randint(part_splits[4], (VIEWS, 4, VIS * BS), 0, P_SIZE), jax.random.fold_in(part_splits[4], 1), 0, P_SIZE - 1).astype(jnp.int32)
    weights = jnp.clip(jnp.exp(math.log(1.0) - 2.9957323 * jax.random.uniform(part_splits[5], (VIEWS, 4, VIS * BS), jnp.float32) ** shard_levels(part_splits[5], (VIEWS, 4, VIS * BS), ((0, 16),), -0.2, 0.2)), 0.05, 1.0)
    return {"embeddings": embeddings, "projection": projection, "owners": owners, "local_blocks": local_blocks, "patches": patches, "weights": weights}


def reference(embeddings, projection, owners, local_blocks, patches, weights):
    sums = jnp.zeros((BLOCKS * BS, D), jnp.float32)
    totals = jnp.zeros((BLOCKS * BS,), jnp.float32)

    def one_view(v, carry):
        sums, totals = carry
        table = embeddings[v]
        index = patches[v]
        wts = weights[v]
        blended = jnp.zeros((VIS * BS, D), jnp.float32)
        for k in range(4):
            blended = blended + wts[k][:, None] * table[index[k]].astype(jnp.float32)
        contrib = jnp.dot(blended.astype(jnp.bfloat16), projection, preferred_element_type=jnp.float32).astype(jnp.bfloat16)
        contrib = lax.optimization_barrier(contrib).astype(jnp.float32)
        block = owners[v, :, 0].astype(jnp.int32) * BLK_DEV + local_blocks[v].astype(jnp.int32)
        rows = (block[:, None] * BS + jnp.arange(BS, dtype=jnp.int32)[None, :]).reshape(-1)
        sums = sums.at[rows].add(contrib)
        totals = totals.at[rows].add(jnp.sum(wts, axis=0))
        return sums, totals

    sums, totals = lax.fori_loop(0, VIEWS, one_view, (sums, totals))
    return (sums / jnp.maximum(totals, 1.0)[:, None]).astype(jnp.bfloat16)
```

```python
import functools

import jax
import jax.numpy as jnp
from jax import lax
from jax.experimental import pallas as pl
from jax.experimental.pallas import tpu as pltpu
from jax.sharding import PartitionSpec as P

BLK_DEV = 64
KERNEL_VIEWS = 16
CHUNK = 128
META_ROWS = 16


def flipped(index, bit):
    return index + bit - 2 * bit * (lax.div(index, bit) % 2)


def gather_sum_kernel(
    emb_ref, proj_ref, meta_ref, out_ref,
    table, sel, place, meta, compact, sums, landed, tots, landed_tots,
    local_sem, meta_send, meta_recv, z_send, z_recv, x_send, x_recv,
    core_send, core_recv, sum_send, sum_recv, tot_send, tot_recv,
):
    npatch = emb_ref.shape[0]
    chunks = table.shape[0]
    rows = meta_ref.shape[2]
    points = place.shape[1]
    group = lax.axis_index("groups")
    me = lax.axis_index("view")
    half = me // 8
    z_peer, x_peer, core_peer = flipped(me, 4), flipped(me, 2), flipped(me, 1)
    half_peers = []
    for r in range(1, 8):
        peer = me
        for bit, axis in ((4, 1), (2, 2), (1, 4)):
            if r & axis:
                peer = flipped(peer, bit)
        half_peers.append(peer)
    across = (me + 8) % KERNEL_VIEWS
    neighbours = half_peers + [across, flipped(across, 4)]
    owner = [((me // 4) % 2) * 8 + e * 4 + me % 4 for e in range(2)]

    def remote(src, dst, send_sem, recv_sem, peer):
        return pltpu.make_async_remote_copy(
            src_ref=src, dst_ref=dst, send_sem=send_sem, recv_sem=recv_sem,
            device_id=(group, peer), device_id_type=pl.DeviceIdType.MESH,
        )

    def own_copy(c):
        cols = pl.ds(pl.multiple_of(c * CHUNK, CHUNK), CHUNK)
        return pltpu.make_async_copy(emb_ref.at[:, cols], table.at[c, 0], local_sem.at[c])

    def z_copy(c):
        return remote(table.at[c, 0], table.at[c, 1], z_send.at[c], z_recv.at[c], z_peer)

    def x_copy(c, j):
        return remote(table.at[c, j], table.at[c, 2 + j], x_send.at[c, j], x_recv.at[c, j], x_peer)

    def core_copy(c, j):
        return remote(
            table.at[c, pl.ds(2 * j, 2)], table.at[c, pl.ds(4 + 2 * j, 2)],
            core_send.at[c, j], core_recv.at[c, j], core_peer,
        )

    def meta_copy(r):
        return remote(
            meta_ref.at[half_peers[r - 1] % 8], meta.at[r], meta_send.at[r], meta_recv.at[r],
            half_peers[r - 1],
        )

    def to_owner(src, dst, send_sem, recv_sem, e, start):
        @pl.when(owner[e] == me)
        def _():
            if start:
                pltpu.make_async_copy(src, dst, recv_sem).start()

        @pl.when(owner[e] != me)
        def _():
            copy = remote(src, dst, send_sem, recv_sem, owner[e])
            if start:
                copy.start()
            else:
                copy.wait_send()

    def sum_copy(c, e, start):
        to_owner(
            sums.at[c, e], landed.at[c, half], sum_send.at[c, e], sum_recv.at[c, half], e, start
        )

    def tot_copy(e, start):
        to_owner(tots.at[e], landed_tots.at[half], tot_send.at[e], tot_recv.at[half], e, start)

    own_meta = pltpu.make_async_copy(meta_ref.at[me % 8], meta.at[0], meta_recv.at[0])
    own_meta.start()
    for c in range(chunks):
        own_copy(c).start()

    barrier = pltpu.get_barrier_semaphore()
    for peer in neighbours:
        pl.semaphore_signal(
            barrier, inc=1, device_id=(group, peer), device_id_type=pl.DeviceIdType.MESH
        )
    pl.semaphore_wait(barrier, len(neighbours))

    for r in range(1, 8):
        meta_copy(r).start()
    for c in range(chunks):
        own_copy(c).wait()
        z_copy(c).start()
        if c < 2:
            x_copy(c, 0).start()

    def forward_z(c):
        z_copy(c).wait_recv()
        x_copy(c, 1).start()
        core_copy(c, 0).start()

    def forward_x(c):
        x_copy(c, 0).wait_recv()
        x_copy(c, 1).wait_recv()
        core_copy(c, 1).start()

    own_meta.wait()
    for r in range(1, 8):
        meta_copy(r).wait_recv()
    patch_ids = lax.broadcasted_iota(jnp.int32, (16, npatch), 1).astype(jnp.float32)

    def build_sel(r):
        @pl.loop(0, 2)
        def _(e):
            block = meta[r, pl.ds(pl.multiple_of(e * META_ROWS, META_ROWS), META_ROWS), :]
            columns = jnp.concatenate(
                [block, jnp.zeros((128 - META_ROWS, rows), jnp.float32)], axis=0
            ).T
            for i in range(rows // 16):
                part = columns[16 * i : 16 * i + 16]
                total = jnp.zeros((16, npatch), jnp.float32)
                for k in range(4):
                    total = total + jnp.where(
                        part[:, k : k + 1] == patch_ids, part[:, 4 + k : 5 + k], 0.0
                    )
                sel[r, pl.ds(pl.multiple_of(e * rows + 16 * i, 16), 16), :] = total.astype(jnp.bfloat16)

    def build_place(e):
        for r in range(8):
            dest = meta[r, e * META_ROWS + 8 : e * META_ROWS + 9, :]
            step = 128

            @pl.loop(0, points // step)
            def _(i):
                start = pl.multiple_of(i * step, step)
                ids = lax.broadcasted_iota(jnp.int32, (step, rows), 0) + start
                place[e, pl.ds(start, step), r * rows : (r + 1) * rows] = jnp.where(
                    ids.astype(jnp.float32) == dest, 1.0, 0.0
                ).astype(jnp.bfloat16)

    forward_z(0)
    pl.loop(0, 4)(build_sel)
    forward_z(1)
    forward_x(0)
    pl.loop(4, 8)(build_sel)
    build_place(0)
    build_place(1)

    row_ids = lax.broadcasted_iota(jnp.int32, (16, rows), 0)
    for e in range(2):
        total = jnp.zeros((16, points), jnp.float32)
        for r in range(8):
            wts = meta[r, e * META_ROWS + 4 : e * META_ROWS + 8, :]
            wts = jnp.sum(wts, axis=0, keepdims=True)
            high = wts.astype(jnp.bfloat16).astype(jnp.float32)
            both = jnp.where(row_ids == 0, high, jnp.where(row_ids == 1, wts - high, 0.0))
            total = total + lax.dot_general(
                both.astype(jnp.bfloat16), place[e, :, r * rows : (r + 1) * rows],
                (((1,), (1,)), ((), ())), preferred_element_type=jnp.float32,
            )
        tots[e] = jnp.broadcast_to(jnp.sum(total, axis=0, keepdims=True), (8, points))
        tot_copy(e, True)

    @pl.loop(0, chunks)
    def _(c):
        @pl.when(c + 2 < chunks)
        def _():
            x_copy(c + 2, 0).start()
            forward_z(c + 2)

        @pl.when(c + 1 < chunks)
        def _():
            forward_x(c + 1)

        core_copy(c, 0).wait_recv()
        core_copy(c, 1).wait_recv()

        @pl.loop(0, 8)
        def _(r):
            blended = jnp.dot(sel[r], table[c, r], preferred_element_type=jnp.float32)
            blended = blended.astype(jnp.bfloat16)
            at = pl.ds(pl.multiple_of(r * rows, rows), rows)
            compact[0, at, :] = blended[:rows]
            compact[1, at, :] = blended[rows:]

        for e in range(2):
            sums[c, e] = jnp.dot(
                place[e], compact[e], preferred_element_type=jnp.float32
            ).astype(jnp.bfloat16)
            sum_copy(c, e, True)

    for h in range(2):
        pltpu.make_async_copy(tots.at[0], landed_tots.at[h], tot_recv.at[h]).wait()
    totals = landed_tots[0] + landed_tots[1]
    totals = jnp.concatenate([totals, jnp.zeros((120, points), jnp.float32)], axis=0).T[:, 0:1]
    parts = []
    for c in range(chunks):
        for h in range(2):
            pltpu.make_async_copy(sums.at[c, 0], landed.at[c, h], sum_recv.at[c, h]).wait()
        parts.append(
            (landed[c, 0].astype(jnp.float32) + landed[c, 1].astype(jnp.float32)).astype(jnp.bfloat16)
        )
    whole = jnp.concatenate(parts, axis=1)
    scaled = jnp.dot(whole, proj_ref[...], preferred_element_type=jnp.float32)
    out_ref[...] = (scaled / jnp.maximum(totals, 1.0)).astype(out_ref.dtype)

    for r in range(1, 8):
        meta_copy(r).wait_send()
    for e in range(2):
        tot_copy(e, False)

    @pl.loop(0, chunks)
    def _(c):
        z_copy(c).wait_send()
        for j in range(2):
            x_copy(c, j).wait_send()
            core_copy(c, j).wait_send()
            sum_copy(c, j, False)


def pack_meta(owners, local_blocks, patches, weights):
    slots = owners.shape[1]
    points = patches.shape[2] // slots
    cap = 2 * slots // KERNEL_VIEWS
    target = owners[0, :, 0]
    slot_ids = jnp.arange(slots, dtype=jnp.int32)
    earlier = slot_ids[None, :] < slot_ids[:, None]
    rank = jnp.sum(((target[:, None] == target[None, :]) & earlier).astype(jnp.int32), axis=1)
    handler = (target // 8) * 4 + target % 4
    position = (handler * 2 + (target // 4) % 2) * cap + rank
    placing = jnp.arange(KERNEL_VIEWS * cap, dtype=jnp.int32)[:, None] == position[None, :]
    dest = local_blocks[0][:, None] * points + jnp.arange(points, dtype=jnp.int32)[None, :] + 1
    values = jnp.concatenate(
        [
            patches[0].reshape(4, slots, points).astype(jnp.float32),
            weights[0].reshape(4, slots, points),
            dest[None].astype(jnp.float32),
        ],
        axis=0,
    )
    packed = jnp.einsum(
        "ksj,ps->kpj", values, placing.astype(jnp.float32), precision=lax.Precision.HIGHEST
    )
    packed = packed.reshape(9, KERNEL_VIEWS, cap * points)
    packed = jnp.concatenate(
        [packed[:8], packed[8:] - 1.0, jnp.zeros((META_ROWS - 9,) + packed.shape[1:], jnp.float32)],
        axis=0,
    )
    return packed.transpose(1, 0, 2).reshape(8, 2 * META_ROWS, cap * points)


def per_device_kernel(embeddings, projection, owners, local_blocks, patches, weights):
    npatch, width = embeddings.shape[1:]
    slots = owners.shape[1]
    points = BLK_DEV * patches.shape[2] // slots
    chunks = width // CHUNK
    meta = pack_meta(owners, local_blocks, patches, weights)
    rows = meta.shape[2]
    bf16, f32 = jnp.bfloat16, jnp.float32
    dma = pltpu.SemaphoreType.DMA
    vmem = pl.BlockSpec(memory_space=pltpu.VMEM)
    return pl.pallas_call(
        gather_sum_kernel,
        out_shape=jax.ShapeDtypeStruct((points, width), bf16),
        in_specs=[pl.BlockSpec(memory_space=pl.ANY), vmem, vmem],
        out_specs=vmem,
        scratch_shapes=[
            pltpu.VMEM((chunks, 8, npatch, CHUNK), bf16),
            pltpu.VMEM((8, 2 * rows, npatch), bf16),
            pltpu.VMEM((2, points, 8 * rows), bf16),
            pltpu.VMEM((8, 2 * META_ROWS, rows), f32),
            pltpu.VMEM((2, 8 * rows, CHUNK), bf16),
            pltpu.VMEM((chunks, 2, points, CHUNK), bf16),
            pltpu.VMEM((chunks, 2, points, CHUNK), bf16),
            pltpu.VMEM((2, 8, points), f32),
            pltpu.VMEM((2, 8, points), f32),
            dma((chunks,)),
            dma((8,)), dma((8,)),
            dma((chunks,)), dma((chunks,)),
            dma((chunks, 2)), dma((chunks, 2)),
            dma((chunks, 2)), dma((chunks, 2)),
            dma((chunks, 2)), dma((chunks, 2)),
            dma((2,)), dma((2,)),
        ],
        compiler_params=pltpu.CompilerParams(
            collective_id=0, has_side_effects=True, vmem_limit_bytes=60 * 1024 * 1024
        ),
    )(embeddings[0], projection, meta)


def per_device(embeddings, projection, owners, local_blocks, patches, weights):
    nview = lax.axis_size("view")
    slots = owners.shape[1]
    width = embeddings.shape[2]
    npatch = embeddings.shape[1]
    points = patches.shape[2] // slots
    blk_count = BLK_DEV
    cap_slots = max(2, 2 * slots // nview)
    table = embeddings[0]
    index = patches[0]
    wts = weights[0]
    patch_ids = jnp.arange(npatch, dtype=jnp.int32)
    selection = jnp.zeros((slots * points, npatch), jnp.float32)
    for k in range(4):
        selection = selection + jnp.where(
            index[k][:, None] == patch_ids[None, :], wts[k][:, None], 0.0
        )
    w_high = selection.astype(jnp.bfloat16)
    w_low = (selection - w_high.astype(jnp.float32)).astype(jnp.bfloat16)
    blended = jnp.dot(w_high, table, preferred_element_type=jnp.float32) + jnp.dot(
        w_low, table, preferred_element_type=jnp.float32
    )
    blended = blended.astype(jnp.bfloat16)
    point_wts = jnp.sum(wts, axis=0).reshape(slots, points)
    target_dev = owners[0, :, 0]
    slot_ids = jnp.arange(slots, dtype=jnp.int32)
    same_owner = target_dev[:, None] == target_dev[None, :]
    earlier = slot_ids[None, :] < slot_ids[:, None]
    rank = jnp.sum((same_owner & earlier).astype(jnp.int32), axis=1)
    position = target_dev * cap_slots + rank
    total_slots = nview * cap_slots
    placing = jnp.arange(total_slots, dtype=jnp.int32)[:, None] == position[None, :]
    send_rows = jnp.dot(
        placing.astype(jnp.bfloat16),
        blended.reshape(slots, points * width),
        preferred_element_type=jnp.float32,
    ).astype(jnp.bfloat16)
    send_wts = jnp.dot(placing.astype(jnp.float32), point_wts, precision=lax.Precision.HIGHEST)
    send_ids = jnp.sum(placing.astype(jnp.int32) * local_blocks[0][None, :], axis=1)
    send_rows = send_rows.reshape(nview, cap_slots, points, width)
    send_wts = send_wts.reshape(nview, cap_slots, points)
    send_ids = send_ids.reshape(nview, cap_slots)
    rows_in = lax.all_to_all(send_rows, "view", split_axis=0, concat_axis=0, tiled=True)
    wts_in = lax.all_to_all(
        send_wts.astype(jnp.bfloat16), "view", split_axis=0, concat_axis=0, tiled=True
    ).astype(send_wts.dtype)
    ids_in = lax.all_to_all(send_ids, "view", split_axis=0, concat_axis=0, tiled=True)
    projected = jnp.einsum(
        "ncsd,de->ncse", rows_in, projection, preferred_element_type=jnp.float32
    ).astype(jnp.bfloat16)
    flat_rows = projected.reshape(total_slots, points * width)
    flat_wts = wts_in.reshape(total_slots, points)
    flat_ids = ids_in.reshape(total_slots)
    selector = jnp.arange(blk_count, dtype=jnp.int32)[:, None] == flat_ids[None, :]
    sums = jnp.dot(selector.astype(jnp.bfloat16), flat_rows, preferred_element_type=jnp.float32)
    totals = jnp.dot(selector.astype(jnp.float32), flat_wts, precision=lax.Precision.HIGHEST)
    sums = sums.reshape(blk_count, points, width)
    scaled = sums / jnp.maximum(totals, 1.0)[:, :, None]
    return scaled.reshape(blk_count * points, width).astype(jnp.bfloat16)


def solution(mesh):
    in_specs = (
        P(("groups", "view"), None, None),
        P(),
        P(("groups", "view"), None, None),
        P(("groups", "view"), None),
        P(("groups", "view"), None, None),
        P(("groups", "view"), None, None),
    )
    out_specs = P(("groups", "view"), None)
    body = per_device_kernel if mesh.shape["view"] == KERNEL_VIEWS else per_device
    return jax.shard_map(
        body, mesh=mesh, in_specs=in_specs, out_specs=out_specs, check_vma=False
    )
```

```python
import functools

import jax
import jax.numpy as jnp
from jax import lax
from jax.experimental import pallas as pl
from jax.experimental.pallas import tpu as pltpu
from jax.sharding import PartitionSpec as P

BLK_DEV = 64
KERNEL_VIEWS = 16
CHUNK = 128
META_ROWS = 16


def flipped(index, bit):
    return index + bit - 2 * bit * (lax.div(index, bit) % 2)


def gather_sum_kernel(
    emb_ref, proj_ref, meta_ref, out_ref,
    table, sel, place, meta, wcols, compact, sums, landed, total, tots, landed_tots,
    local_sem, meta_send, meta_recv, z_send, z_recv, x_send, x_recv,
    core_send, core_recv, sum_send, sum_recv, tot_send, tot_recv,
):
    npatch = emb_ref.shape[0]
    chunks = table.shape[0]
    rows = meta_ref.shape[2]
    points = place.shape[1]
    group = lax.axis_index("groups")
    me = lax.axis_index("view")
    half = me // 8
    z_peer, x_peer, core_peer = flipped(me, 4), flipped(me, 2), flipped(me, 1)
    half_peers = []
    for r in range(1, 8):
        peer = me
        for bit, axis in ((4, 1), (2, 2), (1, 4)):
            if r & axis:
                peer = flipped(peer, bit)
        half_peers.append(peer)
    across = (me + 8) % KERNEL_VIEWS
    neighbours = half_peers + [across, flipped(across, 4)]
    owner = [((me // 4) % 2) * 8 + e * 4 + me % 4 for e in range(2)]

    def remote(src, dst, send_sem, recv_sem, peer):
        return pltpu.make_async_remote_copy(
            src_ref=src, dst_ref=dst, send_sem=send_sem, recv_sem=recv_sem,
            device_id=(group, peer), device_id_type=pl.DeviceIdType.MESH,
        )

    def own_copy(c):
        cols = pl.ds(pl.multiple_of(c * CHUNK, CHUNK), CHUNK)
        return pltpu.make_async_copy(emb_ref.at[:, cols], table.at[c, 0], local_sem.at[c])

    def z_copy(c):
        return remote(table.at[c, 0], table.at[c, 1], z_send.at[c], z_recv.at[c], z_peer)

    def x_copy(c, j):
        return remote(table.at[c, j], table.at[c, 2 + j], x_send.at[c, j], x_recv.at[c, j], x_peer)

    def core_copy(c, j):
        return remote(
            table.at[c, pl.ds(2 * j, 2)], table.at[c, pl.ds(4 + 2 * j, 2)],
            core_send.at[c, j], core_recv.at[c, j], core_peer,
        )

    def meta_copy(r):
        return remote(
            meta_ref.at[half_peers[r - 1] % 8], meta.at[r], meta_send.at[r], meta_recv.at[r],
            half_peers[r - 1],
        )

    def to_owner(src, dst, send_sem, recv_sem, e, start):
        @pl.when(owner[e] == me)
        def _():
            if start:
                pltpu.make_async_copy(src, dst, recv_sem).start()

        @pl.when(owner[e] != me)
        def _():
            copy = remote(src, dst, send_sem, recv_sem, owner[e])
            if start:
                copy.start()
            else:
                copy.wait_send()

    def sum_copy(c, e, start):
        to_owner(
            sums.at[c, e], landed.at[c, half], sum_send.at[c, e], sum_recv.at[c, half], e, start
        )

    def tot_copy(e, start):
        to_owner(tots.at[e], landed_tots.at[half], tot_send.at[e], tot_recv.at[half], e, start)

    own_meta = pltpu.make_async_copy(meta_ref.at[me % 8], meta.at[0], meta_recv.at[0])
    own_meta.start()
    for c in range(chunks):
        own_copy(c).start()

    barrier = pltpu.get_barrier_semaphore()
    for peer in neighbours:
        pl.semaphore_signal(
            barrier, inc=1, device_id=(group, peer), device_id_type=pl.DeviceIdType.MESH
        )
    pl.semaphore_wait(barrier, len(neighbours))

    for r in range(1, 8):
        meta_copy(r).start()
    for c in range(chunks):
        own_copy(c).wait()
        if c < 3:
            z_copy(c).start()
        if c == 0:
            x_copy(c, 0).start()

    def forward_z(c):
        z_copy(c).wait_recv()
        x_copy(c, 1).start()
        core_copy(c, 0).start()

    def forward_x(c):
        x_copy(c, 0).wait_recv()
        x_copy(c, 1).wait_recv()
        core_copy(c, 1).start()

    own_meta.wait()
    for r in range(1, 8):
        meta_copy(r).wait_recv()
    patch_ids = lax.broadcasted_iota(jnp.int32, (16, npatch), 1).astype(jnp.float32)

    def build_sel(r):
        @pl.loop(0, 2)
        def _(e):
            block = meta[r, pl.ds(pl.multiple_of(e * META_ROWS, META_ROWS), META_ROWS), :]
            columns = jnp.concatenate(
                [block, jnp.zeros((128 - META_ROWS, rows), jnp.float32)], axis=0
            ).T
            for i in range(rows // 16):
                part = columns[16 * i : 16 * i + 16]
                total = jnp.zeros((16, npatch), jnp.float32)
                for k in range(4):
                    total = total + jnp.where(
                        part[:, k : k + 1] == patch_ids, part[:, 4 + k : 5 + k], 0.0
                    )
                sel[r, pl.ds(pl.multiple_of(e * rows + 16 * i, 16), 16), :] = total.astype(jnp.bfloat16)
            wts = jnp.sum(columns[:, 4:8], axis=1, keepdims=True)
            high = wts.astype(jnp.bfloat16).astype(jnp.float32)
            lanes = lax.broadcasted_iota(jnp.int32, (rows, CHUNK), 1)
            both = jnp.where(lanes == 0, high, jnp.where(lanes == 1, wts - high, 0.0))
            wcols[e, pl.ds(pl.multiple_of(r * rows, rows), rows), :] = both.astype(jnp.bfloat16)

    def build_place(e):
        for r in range(8):
            dest = meta[r, e * META_ROWS + 8 : e * META_ROWS + 9, :]
            step = 128

            @pl.loop(0, points // step)
            def _(i):
                start = pl.multiple_of(i * step, step)
                ids = lax.broadcasted_iota(jnp.int32, (step, rows), 0) + start
                place[e, pl.ds(start, step), r * rows : (r + 1) * rows] = jnp.where(
                    ids.astype(jnp.float32) == dest, 1.0, 0.0
                ).astype(jnp.bfloat16)

    def project(c):
        for h in range(2):
            pltpu.make_async_copy(sums.at[c, 0], landed.at[c, h], sum_recv.at[c, h]).wait()
        chunk = (landed[c, 0].astype(jnp.float32) + landed[c, 1].astype(jnp.float32)).astype(
            jnp.bfloat16
        )
        at = pl.ds(pl.multiple_of(c * CHUNK, CHUNK), CHUNK)
        return jnp.dot(chunk, proj_ref[at, :], preferred_element_type=jnp.float32)

    pl.loop(0, 3)(build_sel)
    forward_z(0)
    x_copy(1, 0).start()
    pl.loop(3, 8)(build_sel)
    forward_z(1)
    build_place(0)
    build_place(1)
    forward_x(0)

    @pl.loop(0, chunks)
    def _(c):
        @pl.when(c + 3 < chunks)
        def _():
            z_copy(c + 3).start()

        @pl.when(c + 2 < chunks)
        def _():
            x_copy(c + 2, 0).start()
            forward_z(c + 2)

        core_copy(c, 0).wait_recv()
        core_copy(c, 1).wait_recv()

        @pl.loop(0, 8, unroll=4)
        def _(r):
            blended = jnp.dot(sel[r], table[c, r], preferred_element_type=jnp.float32)
            blended = blended.astype(jnp.bfloat16)
            at = pl.ds(pl.multiple_of(r * rows, rows), rows)
            compact[0, at, :] = blended[:rows]
            compact[1, at, :] = blended[rows:]

        for e in range(2):
            sums[c, e] = jnp.dot(
                place[e], compact[e], preferred_element_type=jnp.float32
            ).astype(jnp.bfloat16)
            sum_copy(c, e, True)

        @pl.when(c == 0)
        def _():
            for e in range(2):
                both = jnp.dot(place[e], wcols[e], preferred_element_type=jnp.float32).T
                tots[e] = jnp.broadcast_to(both[0:1] + both[1:2], (8, points))
                tot_copy(e, True)

        @pl.when(c + 1 < chunks)
        def _():
            forward_x(c + 1)

        @pl.when(c == 2)
        def _():
            total[...] = project(0)

        @pl.when(c > 2)
        def _():
            total[...] += project(c - 2)

    for h in range(2):
        pltpu.make_async_copy(tots.at[0], landed_tots.at[h], tot_recv.at[h]).wait()
    totals = landed_tots[0] + landed_tots[1]
    totals = jnp.concatenate([totals, jnp.zeros((120, points), jnp.float32)], axis=0).T[:, 0:1]
    inverse = 1.0 / jnp.maximum(totals, 1.0)
    total[...] += project(chunks - 2)
    out_ref[...] = ((total[...] + project(chunks - 1)) * inverse).astype(out_ref.dtype)

    for r in range(1, 8):
        meta_copy(r).wait_send()
    for e in range(2):
        tot_copy(e, False)

    @pl.loop(0, chunks)
    def _(c):
        z_copy(c).wait_send()
        for j in range(2):
            x_copy(c, j).wait_send()
            core_copy(c, j).wait_send()
            sum_copy(c, j, False)


def pack_meta(owners, local_blocks, patches, weights):
    slots = owners.shape[1]
    points = patches.shape[2] // slots
    cap = 2 * slots // KERNEL_VIEWS
    target = owners[0, :, 0]
    slot_ids = jnp.arange(slots, dtype=jnp.int32)
    earlier = slot_ids[None, :] < slot_ids[:, None]
    rank = jnp.sum(((target[:, None] == target[None, :]) & earlier).astype(jnp.int32), axis=1)
    handler = (target // 8) * 4 + target % 4
    position = (handler * 2 + (target // 4) % 2) * cap + rank
    placing = jnp.arange(KERNEL_VIEWS * cap, dtype=jnp.int32)[:, None] == position[None, :]
    dest = local_blocks[0][:, None] * points + jnp.arange(points, dtype=jnp.int32)[None, :] + 1
    values = jnp.concatenate(
        [
            patches[0].reshape(4, slots, points).astype(jnp.float32),
            weights[0].reshape(4, slots, points),
            dest[None].astype(jnp.float32),
        ],
        axis=0,
    )
    packed = jnp.einsum(
        "ksj,ps->kpj", values, placing.astype(jnp.float32), precision=lax.Precision.HIGHEST
    )
    packed = packed.reshape(9, KERNEL_VIEWS, cap * points)
    packed = jnp.concatenate(
        [packed[:8], packed[8:] - 1.0, jnp.zeros((META_ROWS - 9,) + packed.shape[1:], jnp.float32)],
        axis=0,
    )
    return packed.transpose(1, 0, 2).reshape(8, 2 * META_ROWS, cap * points)


def per_device_kernel(embeddings, projection, owners, local_blocks, patches, weights):
    npatch, width = embeddings.shape[1:]
    slots = owners.shape[1]
    points = BLK_DEV * patches.shape[2] // slots
    chunks = width // CHUNK
    meta = pack_meta(owners, local_blocks, patches, weights)
    rows = meta.shape[2]
    bf16, f32 = jnp.bfloat16, jnp.float32
    dma = pltpu.SemaphoreType.DMA
    vmem = pl.BlockSpec(memory_space=pltpu.VMEM)
    return pl.pallas_call(
        gather_sum_kernel,
        out_shape=jax.ShapeDtypeStruct((points, width), bf16),
        in_specs=[pl.BlockSpec(memory_space=pl.ANY), vmem, vmem],
        out_specs=vmem,
        scratch_shapes=[
            pltpu.VMEM((chunks, 8, npatch, CHUNK), bf16),
            pltpu.VMEM((8, 2 * rows, npatch), bf16),
            pltpu.VMEM((2, points, 8 * rows), bf16),
            pltpu.VMEM((8, 2 * META_ROWS, rows), f32),
            pltpu.VMEM((2, 8 * rows, CHUNK), bf16),
            pltpu.VMEM((2, 8 * rows, CHUNK), bf16),
            pltpu.VMEM((chunks, 2, points, CHUNK), bf16),
            pltpu.VMEM((chunks, 2, points, CHUNK), bf16),
            pltpu.VMEM((points, width), f32),
            pltpu.VMEM((2, 8, points), f32),
            pltpu.VMEM((2, 8, points), f32),
            dma((chunks,)),
            dma((8,)), dma((8,)),
            dma((chunks,)), dma((chunks,)),
            dma((chunks, 2)), dma((chunks, 2)),
            dma((chunks, 2)), dma((chunks, 2)),
            dma((chunks, 2)), dma((chunks, 2)),
            dma((2,)), dma((2,)),
        ],
        compiler_params=pltpu.CompilerParams(
            collective_id=0, has_side_effects=True, vmem_limit_bytes=60 * 1024 * 1024
        ),
    )(embeddings[0], projection, meta)


def per_device(embeddings, projection, owners, local_blocks, patches, weights):
    nview = lax.axis_size("view")
    slots = owners.shape[1]
    width = embeddings.shape[2]
    npatch = embeddings.shape[1]
    points = patches.shape[2] // slots
    blk_count = BLK_DEV
    cap_slots = max(2, 2 * slots // nview)
    table = embeddings[0]
    index = patches[0]
    wts = weights[0]
    patch_ids = jnp.arange(npatch, dtype=jnp.int32)
    selection = jnp.zeros((slots * points, npatch), jnp.float32)
    for k in range(4):
        selection = selection + jnp.where(
            index[k][:, None] == patch_ids[None, :], wts[k][:, None], 0.0
        )
    w_high = selection.astype(jnp.bfloat16)
    w_low = (selection - w_high.astype(jnp.float32)).astype(jnp.bfloat16)
    blended = jnp.dot(w_high, table, preferred_element_type=jnp.float32) + jnp.dot(
        w_low, table, preferred_element_type=jnp.float32
    )
    blended = blended.astype(jnp.bfloat16)
    point_wts = jnp.sum(wts, axis=0).reshape(slots, points)
    target_dev = owners[0, :, 0]
    slot_ids = jnp.arange(slots, dtype=jnp.int32)
    same_owner = target_dev[:, None] == target_dev[None, :]
    earlier = slot_ids[None, :] < slot_ids[:, None]
    rank = jnp.sum((same_owner & earlier).astype(jnp.int32), axis=1)
    position = target_dev * cap_slots + rank
    total_slots = nview * cap_slots
    placing = jnp.arange(total_slots, dtype=jnp.int32)[:, None] == position[None, :]
    send_rows = jnp.dot(
        placing.astype(jnp.bfloat16),
        blended.reshape(slots, points * width),
        preferred_element_type=jnp.float32,
    ).astype(jnp.bfloat16)
    send_wts = jnp.dot(placing.astype(jnp.float32), point_wts, precision=lax.Precision.HIGHEST)
    send_ids = jnp.sum(placing.astype(jnp.int32) * local_blocks[0][None, :], axis=1)
    send_rows = send_rows.reshape(nview, cap_slots, points, width)
    send_wts = send_wts.reshape(nview, cap_slots, points)
    send_ids = send_ids.reshape(nview, cap_slots)
    rows_in = lax.all_to_all(send_rows, "view", split_axis=0, concat_axis=0, tiled=True)
    wts_in = lax.all_to_all(
        send_wts.astype(jnp.bfloat16), "view", split_axis=0, concat_axis=0, tiled=True
    ).astype(send_wts.dtype)
    ids_in = lax.all_to_all(send_ids, "view", split_axis=0, concat_axis=0, tiled=True)
    projected = jnp.einsum(
        "ncsd,de->ncse", rows_in, projection, preferred_element_type=jnp.float32
    ).astype(jnp.bfloat16)
    flat_rows = projected.reshape(total_slots, points * width)
    flat_wts = wts_in.reshape(total_slots, points)
    flat_ids = ids_in.reshape(total_slots)
    selector = jnp.arange(blk_count, dtype=jnp.int32)[:, None] == flat_ids[None, :]
    sums = jnp.dot(selector.astype(jnp.bfloat16), flat_rows, preferred_element_type=jnp.float32)
    totals = jnp.dot(selector.astype(jnp.float32), flat_wts, precision=lax.Precision.HIGHEST)
    sums = sums.reshape(blk_count, points, width)
    scaled = sums / jnp.maximum(totals, 1.0)[:, :, None]
    return scaled.reshape(blk_count * points, width).astype(jnp.bfloat16)


def solution(mesh):
    in_specs = (
        P(("groups", "view"), None, None),
        P(),
        P(("groups", "view"), None, None),
        P(("groups", "view"), None),
        P(("groups", "view"), None, None),
        P(("groups", "view"), None, None),
    )
    out_specs = P(("groups", "view"), None)
    body = per_device_kernel if mesh.shape["view"] == KERNEL_VIEWS else per_device
    return jax.shard_map(
        body, mesh=mesh, in_specs=in_specs, out_specs=out_specs, check_vma=False
    )
```

```python
import functools

import jax
import jax.numpy as jnp
from jax import lax
from jax.experimental import pallas as pl
from jax.experimental.pallas import tpu as pltpu
from jax.sharding import PartitionSpec as P

BLK_DEV = 64
KERNEL_VIEWS = 16
CHUNK = 128
META_ROWS = 16


def flipped(index, bit):
    return index + bit - 2 * bit * (lax.div(index, bit) % 2)


def gather_sum_kernel(
    emb_ref, proj_ref, meta_ref, out_ref,
    table, sel, place, meta, wcols, compact, sums, landed, total, tots, landed_tots,
    local_sem, meta_send, meta_recv, z_send, z_recv, x_send, x_recv,
    core_send, core_recv, sum_send, sum_recv, tot_send, tot_recv,
):
    npatch = emb_ref.shape[0]
    chunks = table.shape[0]
    rows = meta_ref.shape[2]
    points = place.shape[1]
    group = lax.axis_index("groups")
    me = lax.axis_index("view")
    half = me // 8
    z_peer, x_peer, core_peer = flipped(me, 4), flipped(me, 2), flipped(me, 1)
    half_peers = []
    for r in range(1, 8):
        peer = me
        for bit, axis in ((4, 1), (2, 2), (1, 4)):
            if r & axis:
                peer = flipped(peer, bit)
        half_peers.append(peer)
    across = (me + 8) % KERNEL_VIEWS
    neighbours = half_peers + [across, flipped(across, 4)]
    owner = [((me // 4) % 2) * 8 + e * 4 + me % 4 for e in range(2)]

    def remote(src, dst, send_sem, recv_sem, peer):
        return pltpu.make_async_remote_copy(
            src_ref=src, dst_ref=dst, send_sem=send_sem, recv_sem=recv_sem,
            device_id=(group, peer), device_id_type=pl.DeviceIdType.MESH,
        )

    def own_copy(c):
        cols = pl.ds(pl.multiple_of(c * CHUNK, CHUNK), CHUNK)
        return pltpu.make_async_copy(emb_ref.at[:, cols], table.at[c, 0], local_sem.at[c])

    def z_copy(c):
        return remote(table.at[c, 0], table.at[c, 1], z_send.at[c], z_recv.at[c], z_peer)

    def x_copy(c, j):
        return remote(table.at[c, j], table.at[c, 2 + j], x_send.at[c, j], x_recv.at[c, j], x_peer)

    def core_copy(c, j):
        return remote(
            table.at[c, pl.ds(2 * j, 2)], table.at[c, pl.ds(4 + 2 * j, 2)],
            core_send.at[c, j], core_recv.at[c, j], core_peer,
        )

    def meta_copy(r):
        return remote(
            meta_ref.at[half_peers[r - 1] % 8], meta.at[r], meta_send.at[r], meta_recv.at[r],
            half_peers[r - 1],
        )

    def to_owner(src, dst, send_sem, recv_sem, e, start):
        @pl.when(owner[e] == me)
        def _():
            if start:
                pltpu.make_async_copy(src, dst, recv_sem).start()

        @pl.when(owner[e] != me)
        def _():
            copy = remote(src, dst, send_sem, recv_sem, owner[e])
            if start:
                copy.start()
            else:
                copy.wait_send()

    def sum_copy(c, e, start):
        to_owner(
            sums.at[c, e], landed.at[c, half], sum_send.at[c, e], sum_recv.at[c, half], e, start
        )

    def tot_copy(e, start):
        to_owner(tots.at[e], landed_tots.at[half], tot_send.at[e], tot_recv.at[half], e, start)

    own_meta = pltpu.make_async_copy(meta_ref.at[me % 8], meta.at[0], meta_recv.at[0])
    own_meta.start()
    for c in range(chunks):
        own_copy(c).start()

    barrier = pltpu.get_barrier_semaphore()
    for peer in neighbours:
        pl.semaphore_signal(
            barrier, inc=1, device_id=(group, peer), device_id_type=pl.DeviceIdType.MESH
        )
    pl.semaphore_wait(barrier, len(neighbours))

    for r in range(1, 8):
        meta_copy(r).start()
    for c in range(chunks):
        own_copy(c).wait()
        if c < 3:
            z_copy(c).start()
        if c == 0:
            x_copy(c, 0).start()

    def forward_z(c):
        z_copy(c).wait_recv()
        x_copy(c, 1).start()
        core_copy(c, 0).start()

    def forward_x(c):
        x_copy(c, 0).wait_recv()
        x_copy(c, 1).wait_recv()
        core_copy(c, 1).start()

    own_meta.wait()
    for r in range(1, 8):
        meta_copy(r).wait_recv()
    patch_ids = lax.broadcasted_iota(jnp.int32, (16, npatch), 1).astype(jnp.float32)

    def build_sel(r):
        @pl.loop(0, 2)
        def _(e):
            block = meta[r, pl.ds(pl.multiple_of(e * META_ROWS, META_ROWS), META_ROWS), :]
            columns = jnp.concatenate(
                [block, jnp.zeros((128 - META_ROWS, rows), jnp.float32)], axis=0
            ).T
            for i in range(rows // 16):
                part = columns[16 * i : 16 * i + 16]
                total = jnp.zeros((16, npatch), jnp.float32)
                for k in range(4):
                    total = total + jnp.where(
                        part[:, k : k + 1] == patch_ids, part[:, 4 + k : 5 + k], 0.0
                    )
                sel[r, pl.ds(pl.multiple_of(e * rows + 16 * i, 16), 16), :] = total.astype(jnp.bfloat16)
            wts = jnp.sum(columns[:, 4:8], axis=1, keepdims=True)
            high = wts.astype(jnp.bfloat16).astype(jnp.float32)
            lanes = lax.broadcasted_iota(jnp.int32, (rows, CHUNK), 1)
            both = jnp.where(lanes == 0, high, jnp.where(lanes == 1, wts - high, 0.0))
            wcols[e, pl.ds(pl.multiple_of(r * rows, rows), rows), :] = both.astype(jnp.bfloat16)

    def build_place(e):
        for r in range(8):
            dest = meta[r, e * META_ROWS + 8 : e * META_ROWS + 9, :]
            step = 128

            @pl.loop(0, points // step)
            def _(i):
                start = pl.multiple_of(i * step, step)
                ids = lax.broadcasted_iota(jnp.int32, (step, rows), 0) + start
                place[e, pl.ds(start, step), r * rows : (r + 1) * rows] = jnp.where(
                    ids.astype(jnp.float32) == dest, 1.0, 0.0
                ).astype(jnp.bfloat16)

    def project(c):
        for h in range(2):
            pltpu.make_async_copy(sums.at[c, 0], landed.at[c, h], sum_recv.at[c, h]).wait()
        cols = pl.ds(pl.multiple_of(c * CHUNK, CHUNK), CHUNK)

        @pl.loop(0, points // rows)
        def _(i):
            at = pl.ds(pl.multiple_of(i * rows, rows), rows)
            near = landed[c, 0, at, :].astype(jnp.float32)
            chunk = (near + landed[c, 1, at, :].astype(jnp.float32)).astype(jnp.bfloat16)
            total[at, :] += jnp.dot(chunk, proj_ref[cols, :], preferred_element_type=jnp.float32)

    total[...] = jnp.zeros_like(total)
    pl.loop(0, 3)(build_sel)
    forward_z(0)
    x_copy(1, 0).start()
    pl.loop(3, 8)(build_sel)
    forward_z(1)
    build_place(0)
    build_place(1)
    forward_x(0)

    @pl.loop(0, chunks)
    def _(c):
        @pl.when(c + 3 < chunks)
        def _():
            z_copy(c + 3).start()

        @pl.when(c + 2 < chunks)
        def _():
            x_copy(c + 2, 0).start()
            forward_z(c + 2)

        core_copy(c, 0).wait_recv()
        core_copy(c, 1).wait_recv()

        for e in range(2):
            @pl.loop(0, 8)
            def _(r):
                blended = jnp.dot(
                    sel[r, e * rows : (e + 1) * rows], table[c, r], preferred_element_type=jnp.float32
                )
                at = pl.ds(pl.multiple_of(r * rows, rows), rows)
                compact[e, at, :] = blended.astype(jnp.bfloat16)

            sums[c, e] = jnp.dot(
                place[e], compact[e], preferred_element_type=jnp.float32
            ).astype(jnp.bfloat16)
            sum_copy(c, e, True)

        @pl.when(c == 0)
        def _():
            for e in range(2):
                both = jnp.dot(place[e], wcols[e], preferred_element_type=jnp.float32).T
                tots[e] = jnp.broadcast_to(both[0:1] + both[1:2], (8, points))
                tot_copy(e, True)

        @pl.when(c + 1 < chunks)
        def _():
            forward_x(c + 1)

        @pl.when(c >= 2)
        def _():
            project(c - 2)

    for h in range(2):
        pltpu.make_async_copy(tots.at[0], landed_tots.at[h], tot_recv.at[h]).wait()
    totals = landed_tots[0] + landed_tots[1]
    totals = jnp.concatenate([totals, jnp.zeros((120, points), jnp.float32)], axis=0).T[:, 0:1]
    inverse = 1.0 / jnp.maximum(totals, 1.0)
    pl.loop(chunks - 2, chunks)(project)
    out_ref[...] = (total[...] * inverse).astype(out_ref.dtype)

    for r in range(1, 8):
        meta_copy(r).wait_send()
    for e in range(2):
        tot_copy(e, False)

    @pl.loop(0, chunks)
    def _(c):
        z_copy(c).wait_send()
        for j in range(2):
            x_copy(c, j).wait_send()
            core_copy(c, j).wait_send()
            sum_copy(c, j, False)


def pack_meta(owners, local_blocks, patches, weights):
    slots = owners.shape[1]
    points = patches.shape[2] // slots
    cap = 2 * slots // KERNEL_VIEWS
    target = owners[0, :, 0]
    slot_ids = jnp.arange(slots, dtype=jnp.int32)
    earlier = slot_ids[None, :] < slot_ids[:, None]
    rank = jnp.sum(((target[:, None] == target[None, :]) & earlier).astype(jnp.int32), axis=1)
    handler = (target // 8) * 4 + target % 4
    position = (handler * 2 + (target // 4) % 2) * cap + rank
    placing = jnp.arange(KERNEL_VIEWS * cap, dtype=jnp.int32)[:, None] == position[None, :]
    dest = local_blocks[0][:, None] * points + jnp.arange(points, dtype=jnp.int32)[None, :] + 1
    values = jnp.concatenate(
        [
            patches[0].reshape(4, slots, points).astype(jnp.float32),
            weights[0].reshape(4, slots, points),
            dest[None].astype(jnp.float32),
        ],
        axis=0,
    )
    packed = jnp.einsum(
        "ksj,ps->kpj", values, placing.astype(jnp.float32), precision=lax.Precision.HIGHEST
    )
    packed = packed.reshape(9, KERNEL_VIEWS, cap * points)
    packed = jnp.concatenate(
        [packed[:8], packed[8:] - 1.0, jnp.zeros((META_ROWS - 9,) + packed.shape[1:], jnp.float32)],
        axis=0,
    )
    return packed.transpose(1, 0, 2).reshape(8, 2 * META_ROWS, cap * points)


def per_device_kernel(embeddings, projection, owners, local_blocks, patches, weights):
    npatch, width = embeddings.shape[1:]
    slots = owners.shape[1]
    points = BLK_DEV * patches.shape[2] // slots
    chunks = width // CHUNK
    meta = pack_meta(owners, local_blocks, patches, weights)
    rows = meta.shape[2]
    bf16, f32 = jnp.bfloat16, jnp.float32
    dma = pltpu.SemaphoreType.DMA
    vmem = pl.BlockSpec(memory_space=pltpu.VMEM)
    return pl.pallas_call(
        gather_sum_kernel,
        out_shape=jax.ShapeDtypeStruct((points, width), bf16),
        in_specs=[pl.BlockSpec(memory_space=pl.ANY), vmem, vmem],
        out_specs=vmem,
        scratch_shapes=[
            pltpu.VMEM((chunks, 8, npatch, CHUNK), bf16),
            pltpu.VMEM((8, 2 * rows, npatch), bf16),
            pltpu.VMEM((2, points, 8 * rows), bf16),
            pltpu.VMEM((8, 2 * META_ROWS, rows), f32),
            pltpu.VMEM((2, 8 * rows, CHUNK), bf16),
            pltpu.VMEM((2, 8 * rows, CHUNK), bf16),
            pltpu.VMEM((chunks, 2, points, CHUNK), bf16),
            pltpu.VMEM((chunks, 2, points, CHUNK), bf16),
            pltpu.VMEM((points, width), f32),
            pltpu.VMEM((2, 8, points), f32),
            pltpu.VMEM((2, 8, points), f32),
            dma((chunks,)),
            dma((8,)), dma((8,)),
            dma((chunks,)), dma((chunks,)),
            dma((chunks, 2)), dma((chunks, 2)),
            dma((chunks, 2)), dma((chunks, 2)),
            dma((chunks, 2)), dma((chunks, 2)),
            dma((2,)), dma((2,)),
        ],
        compiler_params=pltpu.CompilerParams(
            collective_id=0, has_side_effects=True, vmem_limit_bytes=60 * 1024 * 1024
        ),
    )(embeddings[0], projection, meta)


def per_device(embeddings, projection, owners, local_blocks, patches, weights):
    nview = lax.axis_size("view")
    slots = owners.shape[1]
    width = embeddings.shape[2]
    npatch = embeddings.shape[1]
    points = patches.shape[2] // slots
    blk_count = BLK_DEV
    cap_slots = max(2, 2 * slots // nview)
    table = embeddings[0]
    index = patches[0]
    wts = weights[0]
    patch_ids = jnp.arange(npatch, dtype=jnp.int32)
    selection = jnp.zeros((slots * points, npatch), jnp.float32)
    for k in range(4):
        selection = selection + jnp.where(
            index[k][:, None] == patch_ids[None, :], wts[k][:, None], 0.0
        )
    w_high = selection.astype(jnp.bfloat16)
    w_low = (selection - w_high.astype(jnp.float32)).astype(jnp.bfloat16)
    blended = jnp.dot(w_high, table, preferred_element_type=jnp.float32) + jnp.dot(
        w_low, table, preferred_element_type=jnp.float32
    )
    blended = blended.astype(jnp.bfloat16)
    point_wts = jnp.sum(wts, axis=0).reshape(slots, points)
    target_dev = owners[0, :, 0]
    slot_ids = jnp.arange(slots, dtype=jnp.int32)
    same_owner = target_dev[:, None] == target_dev[None, :]
    earlier = slot_ids[None, :] < slot_ids[:, None]
    rank = jnp.sum((same_owner & earlier).astype(jnp.int32), axis=1)
    position = target_dev * cap_slots + rank
    total_slots = nview * cap_slots
    placing = jnp.arange(total_slots, dtype=jnp.int32)[:, None] == position[None, :]
    send_rows = jnp.dot(
        placing.astype(jnp.bfloat16),
        blended.reshape(slots, points * width),
        preferred_element_type=jnp.float32,
    ).astype(jnp.bfloat16)
    send_wts = jnp.dot(placing.astype(jnp.float32), point_wts, precision=lax.Precision.HIGHEST)
    send_ids = jnp.sum(placing.astype(jnp.int32) * local_blocks[0][None, :], axis=1)
    send_rows = send_rows.reshape(nview, cap_slots, points, width)
    send_wts = send_wts.reshape(nview, cap_slots, points)
    send_ids = send_ids.reshape(nview, cap_slots)
    rows_in = lax.all_to_all(send_rows, "view", split_axis=0, concat_axis=0, tiled=True)
    wts_in = lax.all_to_all(
        send_wts.astype(jnp.bfloat16), "view", split_axis=0, concat_axis=0, tiled=True
    ).astype(send_wts.dtype)
    ids_in = lax.all_to_all(send_ids, "view", split_axis=0, concat_axis=0, tiled=True)
    projected = jnp.einsum(
        "ncsd,de->ncse", rows_in, projection, preferred_element_type=jnp.float32
    ).astype(jnp.bfloat16)
    flat_rows = projected.reshape(total_slots, points * width)
    flat_wts = wts_in.reshape(total_slots, points)
    flat_ids = ids_in.reshape(total_slots)
    selector = jnp.arange(blk_count, dtype=jnp.int32)[:, None] == flat_ids[None, :]
    sums = jnp.dot(selector.astype(jnp.bfloat16), flat_rows, preferred_element_type=jnp.float32)
    totals = jnp.dot(selector.astype(jnp.float32), flat_wts, precision=lax.Precision.HIGHEST)
    sums = sums.reshape(blk_count, points, width)
    scaled = sums / jnp.maximum(totals, 1.0)[:, :, None]
    return scaled.reshape(blk_count * points, width).astype(jnp.bfloat16)


def solution(mesh):
    in_specs = (
        P(("groups", "view"), None, None),
        P(),
        P(("groups", "view"), None, None),
        P(("groups", "view"), None),
        P(("groups", "view"), None, None),
        P(("groups", "view"), None, None),
    )
    out_specs = P(("groups", "view"), None)
    body = per_device_kernel if mesh.shape["view"] == KERNEL_VIEWS else per_device
    return jax.shard_map(
        body, mesh=mesh, in_specs=in_specs, out_specs=out_specs, check_vma=False
    )
```
